32 devices in a mesh: mech: 8 (over z, x), bin: 4 (over y, core).
Axes of the slice: x: 2, y: 2, z: 4, core: 2. Of those that a mesh axis runs over, the one named last changes fastest.
Arguments:
- face_coords: float32 [27, 65536], P(None, ('mech', 'bin')), may hold values from -1.03 to 1.03, as said below
- face_stiff: float32 [65536], P(('mech', 'bin')), may hold values from 1 to 10
- bin_order: int32 [32, 2048], P(('mech', 'bin')), may hold values from 0 to 2047, each once within a row
- slave_pos: float32 [3, 131072], P(None, ('mech', 'bin')), may hold values from -1.3 to 1.3, as said below
- slave_dest: int32 [131072, 1], P(('mech', 'bin')), may hold values from 0 to 31, as said below
- face_slot: int32 [131072], P(('mech', 'bin')), may hold values from 0 to 2047
- block_count: int32 [32, 32], P(('mech', 'bin')), may hold values from 64 to 128
- mirror_face: int32 [65536], P(('mech', 'bin')), may hold values from 0 to 2047
- mirror_node: int32 [65536], P(('mech', 'bin')), may hold values from 0 to 8
- mirror_dest: int32 [65536, 1], P(('mech', 'bin')), may hold values from 0 to 31, as said below
- mirror_slot: int32 [65536], P(('mech', 'bin')), may hold values from 0 to 2047
Outputs:
- slave_force: float32 [3, 131072], P(None, ('mech', 'bin'))
- face_force: float32 [27, 65536], P(None, ('mech', 'bin'))
The draws below stay inside these ranges and needn't reach their ends.
Inputs may be any that keep to these rules, and one draw needn't show every extreme that they name: `face_coords`: node a = i + 3 j of every face lies within 0.03 of (i - 1, j - 1) in its first two components; its third component lies in -0.35 to 0.35. `slave_pos`: first two components lie in -1.3 to 1.3, the third in -0.6 to 0.6. `slave_dest`: among the rows of one device, no bin device is named by more than 256 rows, no element owner holds the named faces of more than 256 rows, and no bin device together with one owner by more than 256 // 4 rows; some bin device and some owner reach 256 from every device. `mirror_dest`: among the rows of one device, no partner device is named by more than 128 rows, no element owner holds the named faces of more than 128 rows, and no partner device together with one owner by more than 128 // 4 rows; some partner device and some owner reach 128 from every device. `bin_order`: each row is a permutation of 0 to 2047.
All inputs are finite; a program needn't handle non-finite values.
Results may differ from the reference program's by a relative error of at most 0.0003.
Values sent between devices are 32-bit elements; how exact they have to be, the bound alone decides.
A program may use at most 64 MiB of HBM per device.

```python
import math
import jax
import jax.numpy as jnp
from jax import lax

F_DEV = 2048
S_DEV = 4096
M_DEV = 2048
NEWTON = 5
FACES = 65536
NODES = 131072
MIRRORS = 65536
SLOT_CAP = 256
MIRROR_CAP = 128
N_MECH = 8
N_BIN = 4
DEVICES = 32


def draw_face_coords(key, part):
    key_plane, key_height = jax.random.split(key, 2)
    entry = jnp.arange(27, dtype=jnp.int32)
    node_id = entry // 3
    component = entry % 3
    grid_x = (node_id % 3 - 1).astype(jnp.float32)
    grid_y = (node_id // 3 - 1).astype(jnp.float32)
    base = jnp.where(component == 0, grid_x, jnp.where(component == 1, grid_y, 0.0))
    planar = jax.random.uniform(key_plane, (27, FACES), jnp.float32, -0.03, 0.03)
    height = jax.random.uniform(key_height, (27, FACES), jnp.float32, -0.35, 0.35)
    values = jnp.where((component == 2)[:, None], height, base[:, None] + planar)
    return values.astype(jnp.float32)


def draw_slave_pos(key, part):
    key_plane, key_depth, key_beyond, key_select = jax.random.split(key, 4)
    plane = jax.random.uniform(key_plane, (2, NODES), jnp.float32, -1.0, 1.0)
    depth = jax.random.uniform(key_depth, (1, NODES), jnp.float32, -0.6, 0.6)
    beyond = jax.random.uniform(key_beyond, (2, NODES), jnp.float32, 1.15, 1.3)
    selected = jax.random.uniform(key_select, (2, NODES), jnp.float32) < 0.02
    plane = jnp.where(selected, jnp.sign(plane) * beyond, plane)
    return jnp.concatenate([plane, depth], 0).astype(jnp.float32)


def pair_layout(key, rows, capacity):
    cell_cap = capacity // N_BIN
    slot_total = DEVICES * capacity
    block_faces = F_DEV // N_BIN
    key_hot, key_source = jax.random.split(key)
    hot_pick = jax.random.randint(key_hot, (2,), 0, DEVICES)
    slot_ids = jnp.arange(slot_total, dtype=jnp.int32)
    cell_id = slot_ids // cell_cap
    dest_dev = cell_id // N_BIN
    face_block = cell_id % N_BIN
    owner_dev = dest_dev // N_BIN * N_BIN + face_block
    forced = ((dest_dev == hot_pick[0]) | (owner_dev == hot_pick[1])).astype(jnp.int32)

    def per_source(source):
        own_key = jax.random.fold_in(key_source, source)
        key_rank, key_rows, key_face = jax.random.split(own_key, 3)
        ranking = jax.random.permutation(key_rank, slot_total).astype(jnp.int32)
        scores = ranking + forced * slot_total
        chosen = lax.top_k(scores, rows)[1]
        chosen = chosen[jax.random.permutation(key_rows, rows)]
        within = jax.random.randint(key_face, (rows,), 0, block_faces)
        return (dest_dev[chosen], face_block[chosen] * block_faces + within)
    targets, places = jax.vmap(per_source)(jnp.arange(DEVICES, dtype=jnp.int32))
    return (targets.reshape(-1).astype(jnp.int32), places.reshape(-1).astype(jnp.int32))


def draw_slave_dest(key, part):
    targets, places = pair_layout(jax.random.fold_in(key, 101), S_DEV, SLOT_CAP)
    return targets[:, None]


def draw_face_slot(key, part):
    targets, places = pair_layout(jax.random.fold_in(key, 101), S_DEV, SLOT_CAP)
    return places


def draw_mirror_dest(key, part):
    targets, places = pair_layout(jax.random.fold_in(key, 202), M_DEV, MIRROR_CAP)
    return targets[:, None]


def draw_mirror_slot(key, part):
    targets, places = pair_layout(jax.random.fold_in(key, 202), M_DEV, MIRROR_CAP)
    return places


def with_ends(entries, key, least, high):
    longest = entries.shape.index(max(entries.shape))
    spots = []
    for shift in (0, 1):
        where = [jax.random.randint(jax.random.fold_in(key, axis), (), 0, length) for axis, length in enumerate(entries.shape)]
        where[longest] = (where[longest] + shift) % entries.shape[longest]
        spots.append(tuple(where))
    return entries.at[spots[0]].set(least).at[spots[1]].set(high)


def levels(key, shape, pieces, least, high):
    def one(position, shards_of):
        heights = jax.random.uniform(jax.random.fold_in(jax.random.fold_in(key, 6), position), (shards_of,), jnp.float32, least / len(pieces), high / len(pieces))
        return jnp.repeat(jnp.exp(heights), shape[position] // shards_of).reshape((-1,) + (1,) * (len(shape) - position - 1))

    gain = one(*pieces[0])
    for cut in pieces[1:]:
        gain = gain * one(*cut)
    return gain


def setup_inputs(seed: int = 0) -> dict:
    key_list = jax.random.split(jax.random.key(seed), 12)
    face_coords = draw_face_coords(jax.random.fold_in(key_list[11], 71), 0)
    face_stiff = jnp.clip(jnp.exp(math.log(10.0) - 2.3025851 * jax.random.uniform(key_list[1], (FACES,), jnp.float32) ** levels(key_list[1], (FACES,), ((0, 32),), -0.2, 0.2)), 1.0, 10.0)
    bin_order = jax.vmap(lambda own: jax.random.permutation(own, F_DEV))(jax.random.split(key_list[2], DEVICES)).reshape((DEVICES, F_DEV)).astype(jnp.int32)
    slave_pos = draw_slave_pos(jax.random.fold_in(key_list[11], 71), 0)
    slave_dest = draw_slave_dest(jax.random.fold_in(key_list[11], 71), 0)
    face_slot = draw_face_slot(jax.random.fold_in(key_list[11], 71), 0)
    block_count = with_ends(jax.random.randint(key_list[6], (DEVICES, S_DEV // 128), 64, 129), jax.random.fold_in(key_list[6], 1), 64, 128).astype(jnp.int32)
    mirror_face = with_ends(jax.random.randint(key_list[7], (MIRRORS,), 0, F_DEV), jax.random.fold_in(key_list[7], 1), 0, F_DEV - 1).astype(jnp.int32)
    mirror_node = with_ends(jax.random.randint(key_list[8], (MIRRORS,), 0, 9), jax.random.fold_in(key_list[8], 1), 0, 8).astype(jnp.int32)
    mirror_dest = draw_mirror_dest(jax.random.fold_in(key_list[11], 71), 0)
    mirror_slot = draw_mirror_slot(jax.random.fold_in(key_list[11], 71), 0)
    return dict(face_coords=face_coords, face_stiff=face_stiff, bin_order=bin_order, slave_pos=slave_pos, slave_dest=slave_dest, face_slot=face_slot, block_count=block_count, mirror_face=mirror_face, mirror_node=mirror_node, mirror_dest=mirror_dest, mirror_slot=mirror_slot)


CLIP_EDGE = 1.1

def lagrange(coord):
    values = (coord * (coord - 1.0) * 0.5, 1.0 - coord * coord, coord * (coord + 1.0) * 0.5)
    slopes = (coord - 0.5, -2.0 * coord, coord + 0.5)
    return (values, slopes)

def shape_table(local_u, local_v):
    val_u, slope_u = lagrange(local_u)
    val_v, slope_v = lagrange(local_v)
    weights = jnp.stack([val_u[i] * val_v[j] for j in range(3) for i in range(3)])
    deriv_u = jnp.stack([slope_u[i] * val_v[j] for j in range(3) for i in range(3)])
    deriv_v = jnp.stack([val_u[i] * slope_v[j] for j in range(3) for i in range(3)])
    return (weights, deriv_u, deriv_v)

def surface_terms(nodes, local_u, local_v):
    weights, deriv_u, deriv_v = shape_table(local_u, local_v)
    surface = lax.optimization_barrier(jnp.sum(weights[:, None, :] * nodes, 0))
    tangent_u = lax.optimization_barrier(jnp.sum(deriv_u[:, None, :] * nodes, 0))
    tangent_v = lax.optimization_barrier(jnp.sum(deriv_v[:, None, :] * nodes, 0))
    return (weights, surface, tangent_u, tangent_v)

def project(points, face_nodes, stiffness, weight):
    count = points.shape[1]
    nodes = face_nodes.reshape(9, 3, count)
    local_u = jnp.zeros((count,), jnp.float32)
    local_v = jnp.zeros((count,), jnp.float32)
    for newton_step in range(NEWTON):
        weights, surface, tangent_u, tangent_v = surface_terms(nodes, local_u, local_v)
        offset = points - surface
        a_uu = lax.optimization_barrier(jnp.sum(tangent_u * tangent_u, 0))
        a_uv = lax.optimization_barrier(jnp.sum(tangent_u * tangent_v, 0))
        a_vv = lax.optimization_barrier(jnp.sum(tangent_v * tangent_v, 0))
        b_u = lax.optimization_barrier(jnp.sum(tangent_u * offset, 0))
        b_v = lax.optimization_barrier(jnp.sum(tangent_v * offset, 0))
        determinant = a_uu * a_vv - a_uv * a_uv
        local_u = jnp.clip(local_u + (a_vv * b_u - a_uv * b_v) / determinant, -CLIP_EDGE, CLIP_EDGE)
        local_v = jnp.clip(local_v + (a_uu * b_v - a_uv * b_u) / determinant, -CLIP_EDGE, CLIP_EDGE)
    weights, surface, tangent_u, tangent_v = surface_terms(nodes, local_u, local_v)
    normal = jnp.stack([tangent_u[1] * tangent_v[2] - tangent_u[2] * tangent_v[1], tangent_u[2] * tangent_v[0] - tangent_u[0] * tangent_v[2], tangent_u[0] * tangent_v[1] - tangent_u[1] * tangent_v[0]])
    normal = normal / jnp.sqrt(lax.optimization_barrier(jnp.sum(normal * normal, 0)))
    penetration = jnp.maximum(-lax.optimization_barrier(jnp.sum((points - surface) * normal, 0)), 0.0)
    contact_force = (0.5 * stiffness * weight * penetration)[None, :] * normal
    reaction = -(weights[:, None, :] * contact_force[None, :, :]).reshape(27, count)
    return (contact_force, reaction)

def reference(face_coords, face_stiff, bin_order, slave_pos, slave_dest, face_slot, block_count, mirror_face, mirror_node, mirror_dest, mirror_slot):
    devices = N_MECH * N_BIN
    block_faces = F_DEV // N_BIN

    def target(dest_dev, slot_index):
        mech_row = dest_dev // N_BIN
        bin_col = dest_dev % N_BIN
        peer = slot_index // block_faces
        within = slot_index % block_faces
        owner = (mech_row * N_BIN + peer).astype(jnp.int32)
        local = bin_order[owner, (bin_col * block_faces + within).astype(jnp.int32)]
        return (owner * F_DEV + local).astype(jnp.int32)

    def visit(carry, inputs):
        owner, points, dests, slots, counts, mfaces, mnodes, mdests, mslots = inputs
        positions = jnp.arange(S_DEV, dtype=jnp.int32)
        live_mask = (positions % 128 < jnp.repeat(counts, 128)).astype(jnp.float32)
        gface = target(dests, slots)
        contact_force, reaction = project(points, face_coords[:, gface], face_stiff[gface], live_mask)
        carry = carry.at[:, gface].add(reaction)
        source = (owner * F_DEV + mfaces).astype(jnp.int32)
        node_rows = (3 * mnodes[None, :] + jnp.arange(3, dtype=jnp.int32)[:, None]).astype(jnp.int32)
        mirror_points = face_coords[node_rows, source[None, :]]
        mface_global = target(mdests, mslots)
        mirror_force, mirror_reaction = project(mirror_points, face_coords[:, mface_global], face_stiff[mface_global], jnp.ones((M_DEV,), jnp.float32))
        carry = carry.at[:, mface_global].add(mirror_reaction)
        carry = carry.at[node_rows, source[None, :]].add(mirror_force)
        return (carry, contact_force)
    inputs = (jnp.arange(devices, dtype=jnp.int32), slave_pos.reshape(3, devices, S_DEV).transpose(1, 0, 2), slave_dest[:, 0].reshape(devices, S_DEV), face_slot.reshape(devices, S_DEV), block_count, mirror_face.reshape(devices, M_DEV), mirror_node.reshape(devices, M_DEV), mirror_dest[:, 0].reshape(devices, M_DEV), mirror_slot.reshape(devices, M_DEV))
    start = jnp.zeros((27, F_DEV * devices), jnp.float32)
    face_force, forces = lax.scan(visit, start, inputs)
    slave_force = forces.transpose(1, 0, 2).reshape(3, S_DEV * devices)
    return (slave_force, face_force)
```

```python
import functools

import jax
import jax.numpy as jnp
from jax import lax
from jax.experimental import pallas as pl
from jax.experimental.pallas import tpu as pltpu
from jax.sharding import PartitionSpec as P

NEWTON = 5
CLIP_EDGE = 1.1
LANES = 128
LOW = 256
F32 = jnp.float32
BF16 = jnp.bfloat16


def iota(shape, axis):
    return lax.broadcasted_iota(jnp.int32, shape, axis)


def whole_part(value, size):
    return jnp.floor((value + 0.5) * (1.0 / size))


def pieces(value):
    high = value.astype(BF16).astype(F32)
    return high, value - high


def hot(mask):
    return jnp.where(mask, 1.0, 0.0).astype(BF16)


def dot_lanes(left, right):
    return lax.dot_general(left, right, (((1,), (1,)), ((), ())), preferred_element_type=F32)


def dot_plain(left, right):
    return lax.dot_general(left, right, (((1,), (0,)), ((), ())), preferred_element_type=F32)


def owner_of(dest, slot, n_bin, block_faces):
    dest = dest.astype(F32)
    slot = slot.astype(F32)
    group = whole_part(dest, n_bin)
    part = whole_part(slot, block_faces)
    owner = group * n_bin + part
    place = (dest - group * n_bin) * block_faces + slot - part * block_faces
    return owner, place


def rank_chunk(owner, seen, tri):
    devices = seen.shape[0]
    width = owner.shape[1]
    mask = iota((devices, width), 0) == owner.astype(jnp.int32)
    ones = jnp.where(mask, 1.0, 0.0)
    earlier = dot_plain(ones.astype(BF16), tri)
    rank = jnp.sum(jnp.where(mask, earlier + seen, 0.0), 0, keepdims=True)
    return rank, seen + jnp.sum(ones, 1, keepdims=True)


def by_group(key, rows8, groups):
    width = rows8.shape[1]
    place = (iota((8, width), 0) >> 2).astype(F32)
    rel = jnp.broadcast_to(key, (8, width)) - place
    return jnp.concatenate(
        [jnp.where(rel == float(2 * j), rows8, 0.0) for j in range(groups // 2)], 0
    )


def spread(key, lane, point, index, groups, lanes):
    width = key.shape[1]
    row = iota((8, width), 0) & 3
    rows8 = jnp.where(
        row == 0, point[0], jnp.where(row == 1, point[1], jnp.where(row == 2, point[2], index))
    )
    onehot = hot(iota((lanes, width), 0) == lane.astype(jnp.int32))
    high, low = pieces(rows8)
    return dot_lanes(by_group(key, high, groups).astype(BF16), onehot) + dot_lanes(
        by_group(key, low, groups).astype(BF16), onehot
    )


def dispatch_kernel(
    n_bin, count, pos, sdest, sslot, coords, mface, mnode, mdest, mslot,
    send_s, send_m, info_s, info_m,
):
    faces = coords.shape[1]
    block_faces = faces // n_bin
    slaves = pos.shape[1]
    mirrors = mface.shape[1]
    lanes = send_s.shape[1]
    devices = send_m.shape[0] // 4
    ratio = send_s.shape[0] // (4 * devices)
    width = 256
    tri = hot(iota((width, width), 0) < iota((width, width), 1))
    seen = jnp.zeros((devices, 1), F32)
    total = jnp.zeros(send_s.shape, F32)
    for step in range(slaves // width):
        cols = pl.ds(step * width, width)
        owner, place = owner_of(sdest[:, cols], sslot[:, cols], n_bin, block_faces)
        spot = iota((1, width), 1)
        limit = jnp.where(
            spot < 128, count[0, 2 * step], count[0, 2 * step + 1]
        )
        live = (spot & 127) < limit
        owner = jnp.where(live, owner, -1.0)
        rank, seen = rank_chunk(owner, seen, tri)
        over = whole_part(rank, lanes)
        key = jnp.where(live, owner * ratio + over, -1.0)
        lane = rank - over * lanes
        info_s[0:1, cols] = key
        info_s[1:2, cols] = lane
        point = [pos[c : c + 1, cols] for c in range(3)]
        total = total + spread(key, lane, point, place + 1.0, ratio * devices, lanes)
    send_s[...] = total

    high_count = faces // LOW
    coord_pieces = pieces(coords[...])
    table = jnp.concatenate(
        [
            jnp.concatenate(
                [
                    jnp.pad(piece[:, h * LOW : (h + 1) * LOW], ((0, 5), (0, 0))).astype(BF16)
                    for h in range(high_count)
                ],
                0,
            )
            for piece in coord_pieces
        ],
        1,
    )
    seen = jnp.zeros((devices, 1), F32)
    total = jnp.zeros(send_m.shape, F32)
    row = iota((32, width), 0)
    for step in range(mirrors // width):
        cols = pl.ds(step * width, width)
        owner, place = owner_of(mdest[:, cols], mslot[:, cols], n_bin, block_faces)
        rank, seen = rank_chunk(owner, seen, tri)
        info_m[0:1, cols] = owner
        info_m[1:2, cols] = rank
        face = mface[:, cols]
        onehot = hot(iota((LOW, width), 0) == (face & (LOW - 1)))
        found = dot_plain(table, jnp.concatenate([onehot, onehot], 0))
        part = face // LOW if LOW & (LOW - 1) else face >> (LOW.bit_length() - 1)
        nodes = jnp.zeros((32, width), F32)
        for h in range(high_count):
            nodes = jnp.where(part == h, found[32 * h : 32 * h + 32], nodes)
        first = 3 * mnode[:, cols]
        point = [
            jnp.sum(jnp.where(row == first + c, nodes, 0.0), 0, keepdims=True) for c in range(3)
        ]
        total = total + spread(owner, rank, point, place + 1.0, devices, lanes)
    send_m[...] = total


def lagrange(t):
    return (
        (t * (t - 1.0) * 0.5, 1.0 - t * t, t * (t + 1.0) * 0.5),
        (t - 0.5, -2.0 * t, t + 0.5),
    )


def surface(nodes, u, v):
    val_u, slope_u = lagrange(u)
    val_v, slope_v = lagrange(v)
    at, along_u, along_v = [], [], []
    for c in range(3):
        line = [sum(val_u[i] * nodes[3 * (i + 3 * j) + c] for i in range(3)) for j in range(3)]
        slope = [sum(slope_u[i] * nodes[3 * (i + 3 * j) + c] for i in range(3)) for j in range(3)]
        at.append(sum(val_v[j] * line[j] for j in range(3)))
        along_u.append(sum(val_v[j] * slope[j] for j in range(3)))
        along_v.append(sum(slope_v[j] * line[j] for j in range(3)))
    return val_u, val_v, at, along_u, along_v


def inner(a, b):
    return a[0] * b[0] + a[1] * b[1] + a[2] * b[2]


def contact(point, nodes, stiff):
    u = jnp.zeros_like(point[0])
    v = jnp.zeros_like(point[0])
    for _ in range(NEWTON):
        _, _, at, tu, tv = surface(nodes, u, v)
        off = [point[c] - at[c] for c in range(3)]
        a_uu, a_uv, a_vv = inner(tu, tu), inner(tu, tv), inner(tv, tv)
        b_u, b_v = inner(tu, off), inner(tv, off)
        inv = 1.0 / (a_uu * a_vv - a_uv * a_uv)
        u = jnp.clip(u + (a_vv * b_u - a_uv * b_v) * inv, -CLIP_EDGE, CLIP_EDGE)
        v = jnp.clip(v + (a_uu * b_v - a_uv * b_u) * inv, -CLIP_EDGE, CLIP_EDGE)
    val_u, val_v, at, tu, tv = surface(nodes, u, v)
    normal = [
        tu[1] * tv[2] - tu[2] * tv[1],
        tu[2] * tv[0] - tu[0] * tv[2],
        tu[0] * tv[1] - tu[1] * tv[0],
    ]
    scale = 1.0 / jnp.sqrt(inner(normal, normal))
    normal = [n * scale for n in normal]
    off = [point[c] - at[c] for c in range(3)]
    press = 0.5 * stiff * jnp.maximum(-inner(off, normal), 0.0)
    force = [press * n for n in normal]
    return force, val_u, val_v


def contact_kernel(
    order, coords, stiff, recv_s, recv_m, ret_s, ret_m, bface,
    pts, forces, react, found, total,
):
    faces = coords.shape[1]
    lanes = recv_s.shape[1]
    devices = recv_m.shape[0] // 4
    ratio = recv_s.shape[0] // (4 * devices)
    rows = (ratio + 1) * devices
    chunks = faces // LANES
    high_count = faces // LOW
    if lanes < LANES:
        pts[...] = jnp.zeros_like(pts)

    def views(c):
        for k in range(ratio + 1):
            for g in range(devices // 8):
                dense = pl.ds(c * rows + k * devices + 8 * g, 8)
                if k < ratio:
                    yield dense, False, pl.ds(g * 32 * ratio + 4 * k + c, 8, stride=4 * ratio)
                else:
                    yield dense, True, pl.ds(g * 32 + c, 8, stride=4)

    for c in range(4):
        for dense, mirror, far in views(c):
            pts[dense, 0:lanes] = (recv_m if mirror else recv_s)[far, :]
    react[pl.ds(27 * rows, 5 * rows), :] = jnp.zeros((5 * rows, LANES), F32)

    def lookup(ref, row, low, high):
        result = None
        for h in range(chunks):
            line = jnp.broadcast_to(ref[row : row + 1, h * LANES : (h + 1) * LANES], (8, LANES))
            value = jnp.take_along_axis(line, low, axis=1, mode="promise_in_bounds")
            result = value if h == 0 else jnp.where(high == h, value, result)
        return result

    def block(i, carry):
        at = pl.multiple_of(i * 8, 8)
        point = [pts[pl.ds(c * rows + at, 8), :] for c in range(3)]
        code = pts[pl.ds(3 * rows + at, 8), :]
        place = jnp.maximum(code - 1.0, 0.0).astype(jnp.int32)
        face = lookup(order, 0, place & (LANES - 1), place >> 7)
        low, high = face & (LANES - 1), face >> 7
        nodes = [lookup(coords, r, low, high) for r in range(27)]
        strength = jnp.where(code > 0.5, lookup(stiff, 0, low, high), 0.0)
        found[pl.ds(at, 8), :] = face
        force, val_u, val_v = contact(point, nodes, strength)
        for c in range(3):
            forces[pl.ds(c * rows + at, 8), :] = force[c]
        for j in range(3):
            for i in range(3):
                weight = -(val_u[i] * val_v[j])
                for c in range(3):
                    row = 3 * (i + 3 * j) + c
                    react[pl.ds(row * rows + at, 8), :] = weight * force[c]
        return carry

    lax.fori_loop(0, rows // 8, block, 0)

    for c in range(3):
        for dense, mirror, far in views(c):
            (ret_m if mirror else ret_s)[far, :] = forces[dense, 0:lanes]
    for dense, mirror, far in views(3):
        (ret_m if mirror else ret_s)[far, :] = jnp.zeros((8, lanes), F32)

    total[...] = jnp.zeros_like(total)

    def add(i, carry):
        lefts, rights = [], []
        for q in range(8):
            p = i * 8 + q
            value = react[pl.ds(p, 32, stride=rows), :]
            upper, lower = pieces(value)
            both = jnp.concatenate([upper.astype(BF16), lower.astype(BF16)], 0)
            face = found[pl.ds(p, 1), :]
            high = jnp.broadcast_to(face >> 8, (16, LANES))
            parts = []
            for h in range(high_count):
                mask = hot(high == h)
                parts.append(both * jnp.concatenate([mask] * 4, 0))
            lefts.append(jnp.concatenate(parts, 0))
            rights.append(hot(iota((LOW, LANES), 0) == (face & (LOW - 1))))
        total[...] += dot_lanes(jnp.concatenate(lefts, 1), jnp.concatenate(rights, 1))
        return carry

    lax.fori_loop(0, rows // 8, add, 0)
    for h in range(high_count):
        bface[:, h * LOW : (h + 1) * LOW] = (
            total[64 * h : 64 * h + 27, :] + total[64 * h + 32 : 64 * h + 59, :]
        )


def fetch(key, lane, table, groups):
    width = key.shape[1]
    lanes = table.shape[1] // 2
    onehot = hot(iota((lanes, width), 0) == lane.astype(jnp.int32))
    spreaded = dot_plain(table, jnp.concatenate([onehot, onehot], 0))
    place = (iota((8, width), 0) >> 2).astype(F32)
    rel = jnp.broadcast_to(key, (8, width)) - place
    result = jnp.zeros((8, width), F32)
    for j in range(groups // 2):
        result = jnp.where(rel == float(2 * j), spreaded[8 * j : 8 * j + 8], result)
    return result + pltpu.roll(result, 4, 0)


def collect_kernel(
    info_s, info_m, mface, mnode, ret_s, ret_m, bface, slave_force, face_force, total
):
    devices = ret_m.shape[0] // 4
    ratio = ret_s.shape[0] // (4 * devices)
    slaves = info_s.shape[1]
    mirrors = info_m.shape[1]
    faces = bface.shape[1]
    high_count = faces // LOW
    width = 256
    table = jnp.concatenate([p.astype(BF16) for p in pieces(ret_s[...])], 1)
    for step in range(slaves // width):
        cols = pl.ds(step * width, width)
        result = fetch(info_s[0:1, cols], info_s[1:2, cols], table, devices * ratio)
        slave_force[:, cols] = result[0:3]
    table = jnp.concatenate([p.astype(BF16) for p in pieces(ret_m[...])], 1)
    acc = None
    for step in range(mirrors // width):
        cols = pl.ds(step * width, width)
        result = fetch(info_m[0:1, cols], info_m[1:2, cols], table, devices)
        face = mface[:, cols]
        key = (face >> 8) * 16 + mnode[:, cols]
        rel = jnp.broadcast_to(key, (8, width)) - (iota((8, width), 0) >> 2)
        left = []
        for piece in pieces(result):
            for h in range(high_count):
                for j in range(5):
                    left.append(jnp.where(rel == 16 * h + 2 * j, piece, 0.0))
        left = jnp.concatenate(left, 0).astype(BF16)
        onehot = hot(iota((LOW, width), 0) == (face & (LOW - 1)))
        term = dot_lanes(left, onehot)
        acc = term if acc is None else acc + term
    total[...] = acc
    half = 40 * high_count
    for h in range(high_count):
        cols = slice(h * LOW, (h + 1) * LOW)
        own = total[40 * h : 40 * h + 40, :] + total[half + 40 * h : half + 40 * h + 40, :]
        for n in range(9):
            face_force[3 * n : 3 * n + 3, cols] = (
                bface[3 * n : 3 * n + 3, cols] + own[4 * n : 4 * n + 3]
            )


def shards(
    face_coords,
    face_stiff,
    bin_order,
    slave_pos,
    slave_dest,
    face_slot,
    block_count,
    mirror_face,
    mirror_node,
    mirror_dest,
    mirror_slot,
):
    n_mech = lax.axis_size("mech")
    n_bin = lax.axis_size("bin")
    devices = n_mech * n_bin
    slaves = slave_pos.shape[1]
    mirrors = mirror_face.shape[0]
    faces = face_coords.shape[1]
    lanes = 2 * mirrors // devices
    ratio = slaves // mirrors
    rows = (ratio + 1) * devices
    vmem = pl.BlockSpec(memory_space=pltpu.VMEM)
    smem = pl.BlockSpec(memory_space=pltpu.SMEM)
    params = pltpu.CompilerParams(vmem_limit_bytes=48 * 2**20)
    shape_s = jax.ShapeDtypeStruct((4 * ratio * devices, lanes), F32)
    shape_m = jax.ShapeDtypeStruct((4 * devices, lanes), F32)
    mface = mirror_face.reshape(1, mirrors)
    mnode = mirror_node.reshape(1, mirrors)
    send_s, send_m, info_s, info_m = pl.pallas_call(
        functools.partial(dispatch_kernel, n_bin),
        out_shape=(
            shape_s,
            shape_m,
            jax.ShapeDtypeStruct((2, slaves), F32),
            jax.ShapeDtypeStruct((2, mirrors), F32),
        ),
        in_specs=[smem] + [vmem] * 8,
        out_specs=(vmem,) * 4,
        compiler_params=params,
        name="dispatch",
    )(
        block_count,
        slave_pos,
        slave_dest.reshape(1, slaves),
        face_slot.reshape(1, slaves),
        face_coords,
        mface,
        mnode,
        mirror_dest.reshape(1, mirrors),
        mirror_slot.reshape(1, mirrors),
    )

    def exchange(value):
        return lax.all_to_all(value, ("mech", "bin"), split_axis=0, concat_axis=0, tiled=True)

    recv_s, recv_m = exchange(send_s), exchange(send_m)
    ret_s, ret_m, bface = pl.pallas_call(
        contact_kernel,
        out_shape=(shape_s, shape_m, jax.ShapeDtypeStruct((27, faces), F32)),
        in_specs=[vmem] * 5,
        out_specs=(vmem,) * 3,
        scratch_shapes=[
            pltpu.VMEM((4 * rows, LANES), F32),
            pltpu.VMEM((3 * rows, LANES), F32),
            pltpu.VMEM((32 * rows, LANES), F32),
            pltpu.VMEM((rows, LANES), jnp.int32),
            pltpu.VMEM((64 * (faces // LOW), LOW), F32),
        ],
        compiler_params=params,
        name="contact",
    )(bin_order, face_coords, face_stiff.reshape(1, faces), recv_s, recv_m)
    back_s, back_m = exchange(ret_s), exchange(ret_m)
    return pl.pallas_call(
        collect_kernel,
        out_shape=(
            jax.ShapeDtypeStruct((3, slaves), F32),
            jax.ShapeDtypeStruct((27, faces), F32),
        ),
        in_specs=[vmem] * 7,
        out_specs=(vmem,) * 2,
        scratch_shapes=[pltpu.VMEM((80 * (faces // LOW), LOW), F32)],
        compiler_params=params,
        name="collect",
    )(info_s, info_m, mface, mnode, back_s, back_m, bface)


def solution(mesh):
    both = ("mech", "bin")
    return jax.shard_map(
        shards,
        mesh=mesh,
        in_specs=(
            P(None, both),
            P(both),
            P(both, None),
            P(None, both),
            P(both, None),
            P(both),
            P(both, None),
            P(both),
            P(both),
            P(both, None),
            P(both),
        ),
        out_specs=(P(None, both), P(None, both)),
        check_vma=False,
    )
```

```python
import functools

import jax
import jax.numpy as jnp
from jax import lax
from jax.experimental import pallas as pl
from jax.experimental.pallas import tpu as pltpu
from jax.sharding import PartitionSpec as P

NEWTON = 5
CLIP_EDGE = 1.1
LANES = 128
LOW = 256
F32 = jnp.float32
BF16 = jnp.bfloat16


def iota(shape, axis):
    return lax.broadcasted_iota(jnp.int32, shape, axis)


def whole_part(value, size):
    return jnp.floor((value + 0.5) * (1.0 / size))


def pieces(value):
    high = value.astype(BF16).astype(F32)
    return high, value - high


def hot(mask):
    return jnp.where(mask, 1.0, 0.0).astype(BF16)


def dot_lanes(left, right):
    return lax.dot_general(left, right, (((1,), (1,)), ((), ())), preferred_element_type=F32)


def dot_plain(left, right):
    return lax.dot_general(left, right, (((1,), (0,)), ((), ())), preferred_element_type=F32)


def owner_of(dest, slot, n_bin, block_faces):
    dest = dest.astype(F32)
    slot = slot.astype(F32)
    group = whole_part(dest, n_bin)
    part = whole_part(slot, block_faces)
    owner = group * n_bin + part
    place = (dest - group * n_bin) * block_faces + slot - part * block_faces
    return owner, place


def rank_chunk(owner, seen, tri):
    devices = seen.shape[0]
    width = owner.shape[1]
    mask = iota((devices, width), 0) == owner.astype(jnp.int32)
    ones = jnp.where(mask, 1.0, 0.0)
    earlier = dot_plain(ones.astype(BF16), tri)
    rank = jnp.sum(jnp.where(mask, earlier + seen, 0.0), 0, keepdims=True)
    return rank, seen + jnp.sum(ones, 1, keepdims=True)


def by_group(key, rows8, groups):
    width = rows8.shape[1]
    group = (iota((4 * groups, width), 0) >> 2).astype(F32)
    return jnp.where(group == key, jnp.concatenate([rows8] * (groups // 2), 0), 0.0)


def spread(key, lane, point, index, groups, lanes):
    width = key.shape[1]
    row = iota((8, width), 0) & 3
    rows8 = jnp.where(
        row == 0, point[0], jnp.where(row == 1, point[1], jnp.where(row == 2, point[2], index))
    )
    onehot = hot(iota((lanes, width), 0) == lane.astype(jnp.int32))
    high, low = pieces(rows8)
    return dot_lanes(by_group(key, high, groups).astype(BF16), onehot) + dot_lanes(
        by_group(key, low, groups).astype(BF16), onehot
    )


def dispatch(n_bin, ratio, count, pos, sdest, sslot, send, info_s, faces):
    faces_bin = faces // n_bin
    devices = send.shape[0]
    slaves = pos.shape[1]
    width = 256
    tri = hot(iota((width, width), 0) < iota((width, width), 1))
    seen = jnp.zeros((devices, 1), F32)
    total = jnp.zeros((4 * ratio * devices, LANES), F32)
    for step in range(slaves // width):
        cols = pl.ds(step * width, width)
        owner, place = owner_of(sdest[:, cols], sslot[:, cols], n_bin, faces_bin)
        spot = iota((1, width), 1)
        limit = jnp.where(
            spot < 128,
            count[0:1, 2 * step : 2 * step + 1],
            count[0:1, 2 * step + 1 : 2 * step + 2],
        )
        live = (spot & 127) < limit
        owner = jnp.where(live, owner, -1.0)
        rank, seen = rank_chunk(owner, seen, tri)
        over = whole_part(rank, LANES)
        key = jnp.where(live, owner * ratio + over, -1.0)
        lane = rank - over * LANES
        info_s[0:1, cols] = key
        info_s[1:2, cols] = lane
        point = [pos[c : c + 1, cols] for c in range(3)]
        total = total + spread(key, lane, point, place + 1.0, ratio * devices, LANES)
    send[:, 0 : 4 * ratio, :] = total.reshape(devices, 4 * ratio, LANES)


def dispatch_mirrors(n_bin, ratio, coords, mface, mnode, mdest, mslot, send, info_m):
    faces = coords.shape[1]
    devices = send.shape[0]
    mirrors = mface.shape[1]
    width = 256
    tri = hot(iota((width, width), 0) < iota((width, width), 1))
    high_count = faces // LOW
    coord_pieces = pieces(coords[...])
    table = jnp.concatenate(
        [
            jnp.concatenate(
                [
                    jnp.pad(piece[:, h * LOW : (h + 1) * LOW], ((0, 5), (0, 0))).astype(BF16)
                    for h in range(high_count)
                ],
                0,
            )
            for piece in coord_pieces
        ],
        1,
    )
    seen = jnp.zeros((devices, 1), F32)
    total = jnp.zeros((4 * devices, LANES), F32)
    row = iota((32, width), 0)
    for step in range(mirrors // width):
        cols = pl.ds(step * width, width)
        owner, place = owner_of(mdest[:, cols], mslot[:, cols], n_bin, faces // n_bin)
        rank, seen = rank_chunk(owner, seen, tri)
        info_m[0:1, cols] = owner
        info_m[1:2, cols] = rank
        face = mface[:, cols]
        onehot = hot(iota((LOW, width), 0) == (face & (LOW - 1)))
        found = dot_plain(table, jnp.concatenate([onehot, onehot], 0))
        part = face >> 8
        nodes = jnp.zeros((32, width), F32)
        for h in range(high_count):
            nodes = jnp.where(part == h, found[32 * h : 32 * h + 32], nodes)
        first = 3 * mnode[:, cols]
        point = [
            jnp.sum(jnp.where(row == first + c, nodes, 0.0), 0, keepdims=True) for c in range(3)
        ]
        total = total + spread(owner, rank, point, place + 1.0, devices, LANES)
    send[:, 4 * ratio : 4 * ratio + 4, :] = total.reshape(devices, 4, LANES)


def lagrange(t):
    return (
        (t * (t - 1.0) * 0.5, 1.0 - t * t, t * (t + 1.0) * 0.5),
        (t - 0.5, -2.0 * t, t + 0.5),
    )


def surface(nodes, u, v):
    val_u, slope_u = lagrange(u)
    val_v, slope_v = lagrange(v)
    at, along_u, along_v = [], [], []
    for c in range(3):
        line = [sum(val_u[i] * nodes[3 * (i + 3 * j) + c] for i in range(3)) for j in range(3)]
        slope = [sum(slope_u[i] * nodes[3 * (i + 3 * j) + c] for i in range(3)) for j in range(3)]
        at.append(sum(val_v[j] * line[j] for j in range(3)))
        along_u.append(sum(val_v[j] * slope[j] for j in range(3)))
        along_v.append(sum(slope_v[j] * line[j] for j in range(3)))
    return val_u, val_v, at, along_u, along_v


def inner(a, b):
    return a[0] * b[0] + a[1] * b[1] + a[2] * b[2]


def contact(point, nodes, stiff):
    u = jnp.zeros_like(point[0])
    v = jnp.zeros_like(point[0])
    for _ in range(NEWTON):
        _, _, at, tu, tv = surface(nodes, u, v)
        off = [point[c] - at[c] for c in range(3)]
        a_uu, a_uv, a_vv = inner(tu, tu), inner(tu, tv), inner(tv, tv)
        b_u, b_v = inner(tu, off), inner(tv, off)
        inv = 1.0 / (a_uu * a_vv - a_uv * a_uv)
        u = jnp.clip(u + (a_vv * b_u - a_uv * b_v) * inv, -CLIP_EDGE, CLIP_EDGE)
        v = jnp.clip(v + (a_uu * b_v - a_uv * b_u) * inv, -CLIP_EDGE, CLIP_EDGE)
    val_u, val_v, at, tu, tv = surface(nodes, u, v)
    normal = [
        tu[1] * tv[2] - tu[2] * tv[1],
        tu[2] * tv[0] - tu[0] * tv[2],
        tu[0] * tv[1] - tu[1] * tv[0],
    ]
    scale = 1.0 / jnp.sqrt(inner(normal, normal))
    normal = [n * scale for n in normal]
    off = [point[c] - at[c] for c in range(3)]
    press = 0.5 * stiff * jnp.maximum(-inner(off, normal), 0.0)
    force = [press * n for n in normal]
    return force, val_u, val_v


def lookup(ref, row, low, high):
    result = None
    for h in range(ref.shape[1] // LANES):
        line = jnp.broadcast_to(ref[row : row + 1, h * LANES : (h + 1) * LANES], (8, LANES))
        value = jnp.take_along_axis(line, low, axis=1, mode="promise_in_bounds")
        result = value if h == 0 else jnp.where(high == h, value, result)
    return result


def contact_block(first, dense, rows, order, coords, stiff, recv, ret, react, found, slot):
    def far(c):
        return pl.ds(first + c, 8, stride=slot)

    point = [recv[far(c), :] for c in range(3)]
    code = recv[far(3), :]
    place = jnp.maximum(code - 1.0, 0.0).astype(jnp.int32)
    face = lookup(order, 0, place & (LANES - 1), place >> 7)
    low, high = face & (LANES - 1), face >> 7
    nodes = [lookup(coords, r, low, high) for r in range(27)]
    strength = jnp.where(code > 0.5, lookup(stiff, 0, low, high), 0.0)
    found[pl.ds(dense, 8), :] = face
    force, val_u, val_v = contact(point, nodes, strength)
    for c in range(3):
        ret[far(c), :] = force[c]
    ret[far(3), :] = jnp.zeros_like(code)
    for j in range(3):
        for i in range(3):
            weight = -(val_u[i] * val_v[j])
            for c in range(3):
                row = 3 * (i + 3 * j) + c
                react[pl.ds(row * rows + dense, 8), :] = weight * force[c]


def scatter(rows, high_count, react, found, total):
    total[...] = jnp.zeros_like(total)

    def add(i, carry):
        lefts, rights = [], []
        for q in range(8):
            p = i * 8 + q
            value = react[pl.ds(p, 32, stride=rows), :]
            upper, lower = pieces(value)
            both = jnp.concatenate([upper.astype(BF16), lower.astype(BF16)], 0)
            face = found[pl.ds(p, 1), :]
            high = jnp.broadcast_to(face >> 8, (16, LANES))
            parts = []
            for h in range(high_count):
                mask = hot(high == h)
                parts.append(both * jnp.concatenate([mask] * 4, 0))
            lefts.append(jnp.concatenate(parts, 0))
            rights.append(hot(iota((LOW, LANES), 0) == (face & (LOW - 1))))
        total[...] += dot_lanes(jnp.concatenate(lefts, 1), jnp.concatenate(rights, 1))
        return carry

    lax.fori_loop(0, rows // 8, add, 0)


def fetch(key, lane, table, groups):
    width = key.shape[1]
    onehot = hot(iota((LANES, width), 0) == lane.astype(jnp.int32))
    spreaded = dot_plain(table, jnp.concatenate([onehot, onehot], 0))
    group = (iota((4 * groups, width), 0) >> 2).astype(F32)
    spreaded = jnp.where(group == key, spreaded, 0.0)
    result = jnp.sum(spreaded.reshape(groups // 2, 8, width), 0)
    return result + pltpu.roll(result, 4, 0)


def piece_table(value):
    return jnp.concatenate([p.astype(BF16) for p in pieces(value)], 1)


def collect(ratio, info_s, info_m, mface, mnode, back, slave_force, face_force, total, own):
    devices = back.shape[0]
    slaves = info_s.shape[1]
    mirrors = info_m.shape[1]
    high_count = face_force.shape[1] // LOW
    width = 256
    table = piece_table(back[:, 4 * ratio : 4 * ratio + 4, :].reshape(4 * devices, LANES))
    acc = None
    for step in range(mirrors // width):
        cols = pl.ds(step * width, width)
        result = fetch(info_m[0:1, cols], info_m[1:2, cols], table, devices)
        face = mface[:, cols]
        key = (face >> 8) * 16 + mnode[:, cols]
        rel = jnp.broadcast_to(key, (8, width)) - (iota((8, width), 0) >> 2)
        left = []
        for piece in pieces(result):
            for h in range(high_count):
                for j in range(5):
                    left.append(jnp.where(rel == 16 * h + 2 * j, piece, 0.0))
        left = jnp.concatenate(left, 0).astype(BF16)
        onehot = hot(iota((LOW, width), 0) == (face & (LOW - 1)))
        term = dot_lanes(left, onehot)
        acc = term if acc is None else acc + term
    own[...] = acc
    half = 40 * high_count
    for h in range(high_count):
        cols = slice(h * LOW, (h + 1) * LOW)
        mine = own[40 * h : 40 * h + 40, :] + own[half + 40 * h : half + 40 * h + 40, :]
        sent = total[64 * h : 64 * h + 27, :] + total[64 * h + 32 : 64 * h + 59, :]
        for n in range(9):
            face_force[3 * n : 3 * n + 3, cols] = (
                sent[3 * n : 3 * n + 3] + mine[4 * n : 4 * n + 3]
            )
    table = piece_table(back[:, 0 : 4 * ratio, :].reshape(4 * ratio * devices, LANES))
    for step in range(slaves // width):
        cols = pl.ds(step * width, width)
        result = fetch(info_s[0:1, cols], info_s[1:2, cols], table, devices * ratio)
        slave_force[:, cols] = result[0:3]


def step_kernel(n_mech, n_bin, ratio, *refs):
    inputs, (slave_force, face_force) = refs[:11], refs[11:13]
    local, rest = refs[13:24], refs[24:]
    (
        send, recv, ret, back, info_s, info_m, react, found, total, own,
        load_sem, go_send, go_recv, home_send, home_recv,
    ) = rest
    devices = n_mech * n_bin
    slot = send.shape[1]
    used = 4 * (ratio + 1)
    rows = (ratio + 1) * devices
    me = lax.axis_index("mech") * n_bin + lax.axis_index("bin")

    def device(i):
        return (i // n_bin, lax.rem(i, n_bin))

    barrier = pltpu.get_barrier_semaphore()

    def greet(i, carry):
        pl.semaphore_signal(
            barrier,
            inc=1,
            device_id=device(lax.rem(me + i, devices)),
            device_id_type=pl.DeviceIdType.MESH,
        )
        return carry

    loads = [
        pltpu.make_async_copy(inputs[n], local[n], load_sem.at[n]) for n in range(len(inputs))
    ]
    for load in loads:
        load.start()
    lax.fori_loop(1, devices, greet, 0)
    (count, pos, sdest, sslot, coords, mface, mnode, mdest, mslot, order, stiff) = local
    faces = coords.shape[1]
    for load in loads:
        load.wait()
    dispatch(n_bin, ratio, count, pos, sdest, sslot, send, info_s, faces)
    dispatch_mirrors(n_bin, ratio, coords, mface, mnode, mdest, mslot, send, info_m)
    pl.semaphore_wait(barrier, devices - 1)

    def go(i):
        target = lax.rem(me + i, devices)
        return pltpu.make_async_remote_copy(
            src_ref=send.at[target, pl.ds(0, used), :],
            dst_ref=recv.at[pl.ds(pl.multiple_of(i * slot, slot), used), :],
            send_sem=go_send.at[i],
            recv_sem=go_recv.at[i],
            device_id=device(target),
            device_id_type=pl.DeviceIdType.MESH,
        )

    def home(i):
        target = lax.rem(me - i + devices, devices)
        return pltpu.make_async_remote_copy(
            src_ref=ret.at[pl.ds(pl.multiple_of(i * slot, slot), used), :],
            dst_ref=back.at[me, pl.ds(0, used), :],
            send_sem=home_send.at[i],
            recv_sem=home_recv.at[i],
            device_id=device(target),
            device_id_type=pl.DeviceIdType.MESH,
        )

    def start_go(i, carry):
        go(i).start()
        return carry

    lax.fori_loop(1, devices, start_go, 0)
    recv[0:used, :] = send[me, 0:used, :]
    react[pl.ds(27 * rows, 5 * rows), :] = jnp.zeros((5 * rows, LANES), F32)

    def group(j, carry):
        for q in range(8):
            i = j * 8 + q

            @pl.when(i > 0)
            def _():
                go(i).wait_recv()

        def block(k, inside):
            first = j * (8 * slot) + 4 * k
            dense = pl.multiple_of((j * (ratio + 1) + k) * 8, 8)
            contact_block(
                first, dense, rows, order, coords, stiff, recv, ret, react, found, slot
            )
            return inside

        lax.fori_loop(0, ratio + 1, block, 0)
        for q in range(8):
            i = j * 8 + q

            @pl.when(i > 0)
            def _():
                home(i).start()

        return carry

    lax.fori_loop(0, devices // 8, group, 0)
    back[me, 0:used, :] = ret[0:used, :]
    scatter(rows, faces // LOW, react, found, total)

    def finish(i, carry):
        go(i).wait_send()
        home(i).wait_send()
        home(i).wait_recv()
        return carry

    lax.fori_loop(1, devices, finish, 0)
    collect(ratio, info_s, info_m, mface, mnode, back, slave_force, face_force, total, own)


def shards(
    face_coords,
    face_stiff,
    bin_order,
    slave_pos,
    slave_dest,
    face_slot,
    block_count,
    mirror_face,
    mirror_node,
    mirror_dest,
    mirror_slot,
):
    n_mech = lax.axis_size("mech")
    n_bin = lax.axis_size("bin")
    devices = n_mech * n_bin
    slaves = slave_pos.shape[1]
    mirrors = mirror_face.shape[0]
    faces = face_coords.shape[1]
    cap = 2 * slaves // devices
    ratio = -(-cap // LANES)
    rows = (ratio + 1) * devices
    slot = 8 * (-(-(ratio + 1) // 2))
    high_count = faces // LOW
    operands = (
        block_count,
        slave_pos,
        slave_dest.reshape(1, slaves),
        face_slot.reshape(1, slaves),
        face_coords,
        mirror_face.reshape(1, mirrors),
        mirror_node.reshape(1, mirrors),
        mirror_dest.reshape(1, mirrors),
        mirror_slot.reshape(1, mirrors),
        bin_order,
        face_stiff.reshape(1, faces),
    )
    vmem = pl.BlockSpec(memory_space=pltpu.VMEM)
    return pl.pallas_call(
        functools.partial(step_kernel, n_mech, n_bin, ratio),
        out_shape=(
            jax.ShapeDtypeStruct((3, slaves), F32),
            jax.ShapeDtypeStruct((27, faces), F32),
        ),
        in_specs=[pl.BlockSpec(memory_space=pltpu.HBM)] * len(operands),
        out_specs=(vmem, vmem),
        scratch_shapes=[pltpu.VMEM(o.shape, o.dtype) for o in operands]
        + [
            pltpu.VMEM((devices, slot, LANES), F32),
            pltpu.VMEM((devices * slot, LANES), F32),
            pltpu.VMEM((devices * slot, LANES), F32),
            pltpu.VMEM((devices, slot, LANES), F32),
            pltpu.VMEM((2, slaves), F32),
            pltpu.VMEM((2, mirrors), F32),
            pltpu.VMEM((32 * rows, LANES), F32),
            pltpu.VMEM((rows, LANES), jnp.int32),
            pltpu.VMEM((64 * high_count, LOW), F32),
            pltpu.VMEM((80 * high_count, LOW), F32),
            pltpu.SemaphoreType.DMA((len(operands),)),
        ]
        + [pltpu.SemaphoreType.DMA((devices,))] * 4,
        compiler_params=pltpu.CompilerParams(
            vmem_limit_bytes=48 * 2**20, collective_id=0, has_side_effects=True
        ),
        name="contact_step",
    )(*operands)


def solution(mesh):
    both = ("mech", "bin")
    return jax.shard_map(
        shards,
        mesh=mesh,
        in_specs=(
            P(None, both),
            P(both),
            P(both, None),
            P(None, both),
            P(both, None),
            P(both),
            P(both, None),
            P(both),
            P(both),
            P(both, None),
            P(both),
        ),
        out_specs=(P(None, both), P(None, both)),
        check_vma=False,
    )
```

```python
import functools

import jax
import jax.numpy as jnp
from jax import lax
from jax.experimental import pallas as pl
from jax.experimental.pallas import tpu as pltpu
from jax.sharding import PartitionSpec as P

NEWTON = 5
CLIP_EDGE = 1.1
LANES = 128
LOW = 256
F32 = jnp.float32
BF16 = jnp.bfloat16


def iota(shape, axis):
    return lax.broadcasted_iota(jnp.int32, shape, axis)


def whole_part(value, size):
    return jnp.floor((value + 0.5) * (1.0 / size))


def pieces(value):
    high = value.astype(BF16).astype(F32)
    return high, value - high


def hot(mask):
    return jnp.where(mask, 1.0, 0.0).astype(BF16)


def dot_lanes(left, right):
    return lax.dot_general(left, right, (((1,), (1,)), ((), ())), preferred_element_type=F32)


def dot_plain(left, right):
    return lax.dot_general(left, right, (((1,), (0,)), ((), ())), preferred_element_type=F32)


def owner_of(dest, slot, n_bin, block_faces):
    dest = dest.astype(F32)
    slot = slot.astype(F32)
    group = whole_part(dest, n_bin)
    part = whole_part(slot, block_faces)
    owner = group * n_bin + part
    place = (dest - group * n_bin) * block_faces + slot - part * block_faces
    return owner, place


def rank_chunk(owner, seen, tri):
    devices = seen.shape[0]
    width = owner.shape[1]
    mask = iota((devices, width), 0) == owner.astype(jnp.int32)
    ones = jnp.where(mask, 1.0, 0.0)
    earlier = dot_plain(ones.astype(BF16), tri)
    rank = jnp.sum(jnp.where(mask, earlier + seen, 0.0), 0, keepdims=True)
    return rank, seen + jnp.sum(ones, 1, keepdims=True)


def by_group(key, rows8, groups):
    width = rows8.shape[1]
    group = (iota((4 * groups, width), 0) >> 2).astype(F32)
    return jnp.where(group == key, jnp.concatenate([rows8] * (groups // 2), 0), 0.0)


def spread(key, lane, point, index, groups, lanes):
    width = key.shape[1]
    row = iota((8, width), 0) & 3
    rows8 = jnp.where(
        row == 0, point[0], jnp.where(row == 1, point[1], jnp.where(row == 2, point[2], index))
    )
    onehot = hot(iota((lanes, width), 0) == lane.astype(jnp.int32))
    high, low = pieces(rows8)
    both = dot_lanes(
        jnp.concatenate(
            [by_group(key, high, groups).astype(BF16), by_group(key, low, groups).astype(BF16)], 0
        ),
        onehot,
    )
    return both[: 4 * groups] + both[4 * groups :]


def dispatch(n_bin, ratio, count, pos, sdest, sslot, send, info_s, faces):
    faces_bin = faces // n_bin
    devices = send.shape[0]
    slaves = pos.shape[1]
    width = 256
    tri = hot(iota((width, width), 0) < iota((width, width), 1))
    seen = jnp.zeros((devices, 1), F32)
    total = jnp.zeros((4 * ratio * devices, LANES), F32)
    for step in range(slaves // width):
        cols = pl.ds(step * width, width)
        owner, place = owner_of(sdest[:, cols], sslot[:, cols], n_bin, faces_bin)
        spot = iota((1, width), 1)
        limit = jnp.where(
            spot < 128,
            count[0:1, 2 * step : 2 * step + 1],
            count[0:1, 2 * step + 1 : 2 * step + 2],
        )
        live = (spot & 127) < limit
        owner = jnp.where(live, owner, -1.0)
        rank, seen = rank_chunk(owner, seen, tri)
        over = whole_part(rank, LANES)
        key = jnp.where(live, owner * ratio + over, -1.0)
        lane = rank - over * LANES
        info_s[0:1, cols] = key
        info_s[1:2, cols] = lane
        point = [pos[c : c + 1, cols] for c in range(3)]
        total = total + spread(key, lane, point, place + 1.0, ratio * devices, LANES)
    send[:, 0 : 4 * ratio, :] = total.reshape(devices, 4 * ratio, LANES)


def dispatch_mirrors(n_bin, ratio, coords, mface, mnode, mdest, mslot, send, info_m):
    faces = coords.shape[1]
    devices = send.shape[0]
    mirrors = mface.shape[1]
    width = 256
    tri = hot(iota((width, width), 0) < iota((width, width), 1))
    high_count = faces // LOW
    coord_pieces = pieces(coords[...])
    table = jnp.concatenate(
        [
            jnp.concatenate(
                [
                    jnp.pad(piece[:, h * LOW : (h + 1) * LOW], ((0, 5), (0, 0))).astype(BF16)
                    for h in range(high_count)
                ],
                0,
            )
            for piece in coord_pieces
        ],
        1,
    )
    seen = jnp.zeros((devices, 1), F32)
    total = jnp.zeros((4 * devices, LANES), F32)
    row = iota((32, width), 0)
    for step in range(mirrors // width):
        cols = pl.ds(step * width, width)
        owner, place = owner_of(mdest[:, cols], mslot[:, cols], n_bin, faces // n_bin)
        rank, seen = rank_chunk(owner, seen, tri)
        info_m[0:1, cols] = owner
        info_m[1:2, cols] = rank
        face = mface[:, cols]
        onehot = hot(iota((LOW, width), 0) == (face & (LOW - 1)))
        found = dot_plain(table, jnp.concatenate([onehot, onehot], 0))
        part = face >> 8
        nodes = jnp.zeros((32, width), F32)
        for h in range(high_count):
            nodes = jnp.where(part == h, found[32 * h : 32 * h + 32], nodes)
        first = 3 * mnode[:, cols]
        point = [
            jnp.sum(jnp.where(row == first + c, nodes, 0.0), 0, keepdims=True) for c in range(3)
        ]
        total = total + spread(owner, rank, point, place + 1.0, devices, LANES)
    send[:, 4 * ratio : 4 * ratio + 4, :] = total.reshape(devices, 4, LANES)


def lagrange(t):
    return (
        (t * (t - 1.0) * 0.5, 1.0 - t * t, t * (t + 1.0) * 0.5),
        (t - 0.5, -2.0 * t, t + 0.5),
    )


def surface(nodes, u, v):
    val_u, slope_u = lagrange(u)
    val_v, slope_v = lagrange(v)
    at, along_u, along_v = [], [], []
    for c in range(3):
        line = [sum(val_u[i] * nodes[3 * (i + 3 * j) + c] for i in range(3)) for j in range(3)]
        slope = [sum(slope_u[i] * nodes[3 * (i + 3 * j) + c] for i in range(3)) for j in range(3)]
        at.append(sum(val_v[j] * line[j] for j in range(3)))
        along_u.append(sum(val_v[j] * slope[j] for j in range(3)))
        along_v.append(sum(slope_v[j] * line[j] for j in range(3)))
    return val_u, val_v, at, along_u, along_v


def inner(a, b):
    return a[0] * b[0] + a[1] * b[1] + a[2] * b[2]


def contact(point, nodes, stiff):
    u = jnp.zeros_like(point[0])
    v = jnp.zeros_like(point[0])
    for _ in range(NEWTON):
        _, _, at, tu, tv = surface(nodes, u, v)
        off = [point[c] - at[c] for c in range(3)]
        a_uu, a_uv, a_vv = inner(tu, tu), inner(tu, tv), inner(tv, tv)
        b_u, b_v = inner(tu, off), inner(tv, off)
        inv = 1.0 / (a_uu * a_vv - a_uv * a_uv)
        u = jnp.clip(u + (a_vv * b_u - a_uv * b_v) * inv, -CLIP_EDGE, CLIP_EDGE)
        v = jnp.clip(v + (a_uu * b_v - a_uv * b_u) * inv, -CLIP_EDGE, CLIP_EDGE)
    val_u, val_v, at, tu, tv = surface(nodes, u, v)
    normal = [
        tu[1] * tv[2] - tu[2] * tv[1],
        tu[2] * tv[0] - tu[0] * tv[2],
        tu[0] * tv[1] - tu[1] * tv[0],
    ]
    scale = 1.0 / jnp.sqrt(inner(normal, normal))
    normal = [n * scale for n in normal]
    off = [point[c] - at[c] for c in range(3)]
    press = 0.5 * stiff * jnp.maximum(-inner(off, normal), 0.0)
    force = [press * n for n in normal]
    return force, val_u, val_v


def lookup(ref, row, low, high):
    result = None
    for h in range(ref.shape[1] // LANES):
        line = jnp.broadcast_to(ref[row : row + 1, h * LANES : (h + 1) * LANES], (8, LANES))
        value = [
            jnp.take_along_axis(line, part, axis=1, mode="promise_in_bounds") for part in low
        ]
        if h == 0:
            result = value
        else:
            result = [jnp.where(hi == h, v, r) for hi, v, r in zip(high, value, result)]
    return result


def contact_blocks(blocks, rows, order, coords, stiff, recv, ret, react, found, slot):
    def split(value):
        return [value[8 * n : 8 * n + 8] for n in range(len(blocks))]

    def far(first, c):
        return pl.ds(first + c, 8, stride=slot)

    def taken(c):
        return jnp.concatenate([recv[far(first, c), :] for first, dense in blocks], 0)

    def looked(ref, row, index):
        low = split(index & (LANES - 1))
        return jnp.concatenate(lookup(ref, row, low, split(index >> 7)), 0)

    point = [taken(c) for c in range(3)]
    code = taken(3)
    place = jnp.maximum(code - 1.0, 0.0).astype(jnp.int32)
    face = looked(order, 0, place)
    nodes = [looked(coords, r, face) for r in range(27)]
    strength = jnp.where(code > 0.5, looked(stiff, 0, face), 0.0)
    force, val_u, val_v = contact(point, nodes, strength)
    for n, (first, dense) in enumerate(blocks):
        part = slice(8 * n, 8 * n + 8)
        found[pl.ds(dense, 8), :] = face[part]
        for c in range(3):
            ret[far(first, c), :] = force[c][part]
        ret[far(first, 3), :] = jnp.zeros((8, LANES), F32)
    for j in range(3):
        for i in range(3):
            weight = -(val_u[i] * val_v[j])
            for c in range(3):
                row = 3 * (i + 3 * j) + c
                term = weight * force[c]
                for n, (first, dense) in enumerate(blocks):
                    react[pl.ds(row * rows + dense, 8), :] = term[8 * n : 8 * n + 8]


def scatter(rows, high_count, react, found, total):
    total[...] = jnp.zeros_like(total)

    def add(i, carry):
        lefts, rights = [], []
        for q in range(8):
            p = i * 8 + q
            value = react[pl.ds(p, 32, stride=rows), :]
            upper, lower = pieces(value)
            both = jnp.concatenate([upper.astype(BF16), lower.astype(BF16)], 0)
            face = found[pl.ds(p, 1), :]
            high = jnp.broadcast_to(face >> 8, (16, LANES))
            parts = []
            for h in range(high_count):
                mask = hot(high == h)
                parts.append(both * jnp.concatenate([mask] * 4, 0))
            lefts.append(jnp.concatenate(parts, 0))
            rights.append(hot(iota((LOW, LANES), 0) == (face & (LOW - 1))))
        total[...] += dot_lanes(jnp.concatenate(lefts, 1), jnp.concatenate(rights, 1))
        return carry

    lax.fori_loop(0, rows // 8, add, 0)


def fetch(key, lane, table, groups):
    width = key.shape[1]
    onehot = hot(iota((LANES, width), 0) == lane.astype(jnp.int32))
    spreaded = dot_plain(table, jnp.concatenate([onehot, onehot], 0))
    group = (iota((4 * groups, width), 0) >> 2).astype(F32)
    spreaded = jnp.where(group == key, spreaded, 0.0)
    result = jnp.sum(spreaded.reshape(groups // 2, 8, width), 0)
    return result + pltpu.roll(result, 4, 0)


def piece_table(value):
    return jnp.concatenate([p.astype(BF16) for p in pieces(value)], 1)


def collect(ratio, info_s, info_m, mface, mnode, back, slave_force, face_force, total, own):
    devices = back.shape[0]
    slaves = info_s.shape[1]
    mirrors = info_m.shape[1]
    high_count = face_force.shape[1] // LOW
    width = 256
    table = piece_table(back[:, 4 * ratio : 4 * ratio + 4, :].reshape(4 * devices, LANES))
    acc = None
    for step in range(mirrors // width):
        cols = pl.ds(step * width, width)
        result = fetch(info_m[0:1, cols], info_m[1:2, cols], table, devices)
        face = mface[:, cols]
        key = (face >> 8) * 16 + mnode[:, cols]
        rel = jnp.broadcast_to(key, (8, width)) - (iota((8, width), 0) >> 2)
        left = []
        for piece in pieces(result):
            for h in range(high_count):
                for j in range(5):
                    left.append(jnp.where(rel == 16 * h + 2 * j, piece, 0.0))
        left = jnp.concatenate(left, 0).astype(BF16)
        onehot = hot(iota((LOW, width), 0) == (face & (LOW - 1)))
        term = dot_lanes(left, onehot)
        acc = term if acc is None else acc + term
    own[...] = acc
    half = 40 * high_count
    for h in range(high_count):
        cols = slice(h * LOW, (h + 1) * LOW)
        mine = own[40 * h : 40 * h + 40, :] + own[half + 40 * h : half + 40 * h + 40, :]
        sent = total[64 * h : 64 * h + 27, :] + total[64 * h + 32 : 64 * h + 59, :]
        for n in range(9):
            face_force[3 * n : 3 * n + 3, cols] = (
                sent[3 * n : 3 * n + 3] + mine[4 * n : 4 * n + 3]
            )
    table = piece_table(back[:, 0 : 4 * ratio, :].reshape(4 * ratio * devices, LANES))
    for step in range(slaves // width):
        cols = pl.ds(step * width, width)
        result = fetch(info_s[0:1, cols], info_s[1:2, cols], table, devices * ratio)
        slave_force[:, cols] = result[0:3]


def step_kernel(n_mech, n_bin, ratio, *refs):
    inputs, (slave_force, face_force) = refs[:11], refs[11:13]
    local, rest = refs[13:24], refs[24:]
    (
        send, recv, ret, back, info_s, info_m, react, found, total, own,
        load_sem, go_send, go_recv, home_send, home_recv,
    ) = rest
    devices = n_mech * n_bin
    slot = send.shape[1]
    used = 4 * (ratio + 1)
    rows = (ratio + 1) * devices
    me = lax.axis_index("mech") * n_bin + lax.axis_index("bin")

    def device(i):
        return (i // n_bin, lax.rem(i, n_bin))

    barrier = pltpu.get_barrier_semaphore()

    def greet(i, carry):
        pl.semaphore_signal(
            barrier,
            inc=1,
            device_id=device(lax.rem(me + i, devices)),
            device_id_type=pl.DeviceIdType.MESH,
        )
        return carry

    loads = [
        pltpu.make_async_copy(inputs[n], local[n], load_sem.at[n]) for n in range(len(inputs))
    ]
    for load in loads:
        load.start()
    lax.fori_loop(1, devices, greet, 0)
    (count, pos, sdest, sslot, coords, mface, mnode, mdest, mslot, order, stiff) = local
    faces = coords.shape[1]
    for load in loads:
        load.wait()
    dispatch(n_bin, ratio, count, pos, sdest, sslot, send, info_s, faces)
    pl.semaphore_wait(barrier, devices - 1)
    halves = ((0, 4 * ratio), (4 * ratio, 4))

    def go(i, half):
        target = lax.rem(me + i, devices)
        start, size = halves[half]
        return pltpu.make_async_remote_copy(
            src_ref=send.at[target, pl.ds(start, size), :],
            dst_ref=recv.at[pl.ds(pl.multiple_of(i * slot, slot) + start, size), :],
            send_sem=go_send.at[half, i],
            recv_sem=go_recv.at[half, i],
            device_id=device(target),
            device_id_type=pl.DeviceIdType.MESH,
        )

    def home(i, half):
        target = lax.rem(me - i + devices, devices)
        start, size = halves[half]
        return pltpu.make_async_remote_copy(
            src_ref=ret.at[pl.ds(pl.multiple_of(i * slot, slot) + start, size), :],
            dst_ref=back.at[me, pl.ds(start, size), :],
            send_sem=home_send.at[half, i],
            recv_sem=home_recv.at[half, i],
            device_id=device(target),
            device_id_type=pl.DeviceIdType.MESH,
        )

    def start_go(half):
        def start(i, carry):
            go(i, half).start()
            return carry

        lax.fori_loop(1, devices, start, 0)

    start_go(0)
    dispatch_mirrors(n_bin, ratio, coords, mface, mnode, mdest, mslot, send, info_m)
    start_go(1)
    recv[0:used, :] = send[me, 0:used, :]
    react[pl.ds(27 * rows, 5 * rows), :] = jnp.zeros((5 * rows, LANES), F32)
    tables = (rows, order, coords, stiff, recv, ret, react, found, slot)

    def peers(j, count, act):
        for q in range(count):
            i = j * count + q

            @pl.when(i > 0)
            def _():
                act(i)

    def group(j, carry):
        peers(j, 8, lambda i: go(i, 0).wait_recv())
        blocks = [
            (j * (8 * slot) + 4 * k, pl.multiple_of((j * ratio + k) * 8, 8)) for k in range(ratio)
        ]
        contact_blocks(blocks, *tables)
        peers(j, 8, lambda i: home(i, 0).start())
        return carry

    lax.fori_loop(0, devices // 8, group, 0)
    pair = 2 if devices % 16 == 0 else 1

    def mirror_group(j, carry):
        peers(j, 8 * pair, lambda i: go(i, 1).wait_recv())
        blocks = []
        for k in range(pair):
            g = j * pair + k
            dense = pl.multiple_of(ratio * devices + g * 8, 8)
            blocks.append((g * (8 * slot) + 4 * ratio, dense))
        contact_blocks(blocks, *tables)
        peers(j, 8 * pair, lambda i: home(i, 1).start())
        return carry

    lax.fori_loop(0, devices // (8 * pair), mirror_group, 0)
    back[me, 0:used, :] = ret[0:used, :]
    scatter(rows, faces // LOW, react, found, total)

    def finish(i, carry):
        for half in range(2):
            go(i, half).wait_send()
            home(i, half).wait_send()
            home(i, half).wait_recv()
        return carry

    lax.fori_loop(1, devices, finish, 0)
    collect(ratio, info_s, info_m, mface, mnode, back, slave_force, face_force, total, own)


def shards(
    face_coords,
    face_stiff,
    bin_order,
    slave_pos,
    slave_dest,
    face_slot,
    block_count,
    mirror_face,
    mirror_node,
    mirror_dest,
    mirror_slot,
):
    n_mech = lax.axis_size("mech")
    n_bin = lax.axis_size("bin")
    devices = n_mech * n_bin
    slaves = slave_pos.shape[1]
    mirrors = mirror_face.shape[0]
    faces = face_coords.shape[1]
    cap = 2 * slaves // devices
    ratio = -(-cap // LANES)
    rows = (ratio + 1) * devices
    slot = 8 * (-(-(ratio + 1) // 2))
    high_count = faces // LOW
    operands = (
        block_count,
        slave_pos,
        slave_dest.reshape(1, slaves),
        face_slot.reshape(1, slaves),
        face_coords,
        mirror_face.reshape(1, mirrors),
        mirror_node.reshape(1, mirrors),
        mirror_dest.reshape(1, mirrors),
        mirror_slot.reshape(1, mirrors),
        bin_order,
        face_stiff.reshape(1, faces),
    )
    vmem = pl.BlockSpec(memory_space=pltpu.VMEM)
    return pl.pallas_call(
        functools.partial(step_kernel, n_mech, n_bin, ratio),
        out_shape=(
            jax.ShapeDtypeStruct((3, slaves), F32),
            jax.ShapeDtypeStruct((27, faces), F32),
        ),
        in_specs=[pl.BlockSpec(memory_space=pltpu.HBM)] * len(operands),
        out_specs=(vmem, vmem),
        scratch_shapes=[pltpu.VMEM(o.shape, o.dtype) for o in operands]
        + [
            pltpu.VMEM((devices, slot, LANES), F32),
            pltpu.VMEM((devices * slot, LANES), F32),
            pltpu.VMEM((devices * slot, LANES), F32),
            pltpu.VMEM((devices, slot, LANES), F32),
            pltpu.VMEM((2, slaves), F32),
            pltpu.VMEM((2, mirrors), F32),
            pltpu.VMEM((32 * rows, LANES), F32),
            pltpu.VMEM((rows, LANES), jnp.int32),
            pltpu.VMEM((64 * high_count, LOW), F32),
            pltpu.VMEM((80 * high_count, LOW), F32),
            pltpu.SemaphoreType.DMA((len(operands),)),
        ]
        + [pltpu.SemaphoreType.DMA((2, devices))] * 4,
        compiler_params=pltpu.CompilerParams(
            vmem_limit_bytes=63 * 2**20, collective_id=0, has_side_effects=True
        ),
        name="contact_step",
    )(*operands)


def solution(mesh):
    both = ("mech", "bin")
    return jax.shard_map(
        shards,
        mesh=mesh,
        in_specs=(
            P(None, both),
            P(both),
            P(both, None),
            P(None, both),
            P(both, None),
            P(both),
            P(both, None),
            P(both),
            P(both),
            P(both, None),
            P(both),
        ),
        out_specs=(P(None, both), P(None, both)),
        check_vma=False,
    )
```

```python
import functools

import jax
import jax.numpy as jnp
from jax import lax
from jax.experimental import pallas as pl
from jax.experimental.pallas import tpu as pltpu
from jax.sharding import PartitionSpec as P

NEWTON = 5
CLIP_EDGE = 1.1
LANES = 128
LOW = 256
F32 = jnp.float32
BF16 = jnp.bfloat16


def iota(shape, axis):
    return lax.broadcasted_iota(jnp.int32, shape, axis)


def whole_part(value, size):
    return jnp.floor((value + 0.5) * (1.0 / size))


def pieces(value):
    high = value.astype(BF16).astype(F32)
    return high, value - high


def hot(mask):
    return jnp.where(mask, 1.0, 0.0).astype(BF16)


def counted(shape):
    return iota(shape, 0).astype(F32).astype(BF16)


def hot_rows(numbers, row):
    wide = jnp.broadcast_to(row.astype(F32), (16, row.shape[1])).astype(BF16)
    wide = jnp.concatenate([wide] * (numbers.shape[0] // 16), 0)
    return jnp.where(numbers == wide, jnp.ones_like(wide), jnp.zeros_like(wide))


def dot_lanes(left, right):
    return lax.dot_general(left, right, (((1,), (1,)), ((), ())), preferred_element_type=F32)


def dot_plain(left, right):
    return lax.dot_general(left, right, (((1,), (0,)), ((), ())), preferred_element_type=F32)


def owner_of(dest, slot, n_bin, block_faces):
    dest = dest.astype(F32)
    slot = slot.astype(F32)
    group = whole_part(dest, n_bin)
    part = whole_part(slot, block_faces)
    owner = group * n_bin + part
    place = (dest - group * n_bin) * block_faces + slot - part * block_faces
    return owner, place


def rank_chunk(owner, seen, tri):
    devices = seen.shape[0]
    width = owner.shape[1]
    mask = iota((devices, width), 0) == owner.astype(jnp.int32)
    ones = jnp.where(mask, 1.0, 0.0)
    earlier = dot_plain(ones.astype(BF16), tri)
    rank = jnp.sum(jnp.where(mask, earlier + seen, 0.0), 0, keepdims=True)
    return rank, seen + jnp.sum(ones, 1, keepdims=True)


def by_group(key, rows8, groups):
    width = rows8.shape[1]
    group = (iota((4 * groups, width), 0) >> 2).astype(F32).astype(BF16)
    wide = jnp.broadcast_to(key, (16, width)).astype(BF16)
    wide = jnp.concatenate([wide] * (groups // 4), 0)
    rows16 = jnp.concatenate([rows8, rows8], 0).astype(BF16)
    rows16 = jnp.concatenate([rows16] * (groups // 4), 0)
    return jnp.where(group == wide, rows16, jnp.zeros_like(rows16))


def spread(key, lane, point, index, groups, lanes):
    width = key.shape[1]
    row = iota((8, width), 0) & 3
    rows8 = jnp.where(
        row == 0, point[0], jnp.where(row == 1, point[1], jnp.where(row == 2, point[2], index))
    )
    onehot = hot_rows(counted((lanes, width)), lane)
    high, low = pieces(rows8)
    both = dot_lanes(
        jnp.concatenate(
            [by_group(key, high, groups), by_group(key, low, groups)], 0
        ),
        onehot,
    )
    return both[: 4 * groups] + both[4 * groups :]


def dispatch(n_bin, ratio, count, pos, sdest, sslot, send, info_s, faces):
    faces_bin = faces // n_bin
    devices = send.shape[0]
    slaves = pos.shape[1]
    width = 256
    tri = hot(iota((width, width), 0) < iota((width, width), 1))
    seen = jnp.zeros((devices, 1), F32)
    total = jnp.zeros((4 * ratio * devices, LANES), F32)
    for step in range(slaves // width):
        cols = pl.ds(step * width, width)
        owner, place = owner_of(sdest[:, cols], sslot[:, cols], n_bin, faces_bin)
        spot = iota((1, width), 1)
        limit = jnp.where(
            spot < 128,
            count[0:1, 2 * step : 2 * step + 1],
            count[0:1, 2 * step + 1 : 2 * step + 2],
        )
        live = (spot & 127) < limit
        owner = jnp.where(live, owner, -1.0)
        rank, seen = rank_chunk(owner, seen, tri)
        over = whole_part(rank, LANES)
        key = jnp.where(live, owner * ratio + over, -1.0)
        lane = rank - over * LANES
        info_s[0:1, cols] = key
        info_s[1:2, cols] = lane
        point = [pos[c : c + 1, cols] for c in range(3)]
        total = total + spread(key, lane, point, place + 1.0, ratio * devices, LANES)
    send[:, 0 : 4 * ratio, :] = total.reshape(devices, 4 * ratio, LANES)


def dispatch_mirrors(n_bin, ratio, coords, mface, mnode, mdest, mslot, send, info_m):
    faces = coords.shape[1]
    devices = send.shape[0]
    mirrors = mface.shape[1]
    width = 256
    tri = hot(iota((width, width), 0) < iota((width, width), 1))
    high_count = faces // LOW
    coord_pieces = pieces(coords[...])
    table = jnp.concatenate(
        [
            jnp.concatenate(
                [
                    jnp.pad(piece[:, h * LOW : (h + 1) * LOW], ((0, 5), (0, 0))).astype(BF16)
                    for h in range(high_count)
                ],
                0,
            )
            for piece in coord_pieces
        ],
        1,
    )
    seen = jnp.zeros((devices, 1), F32)
    total = jnp.zeros((4 * devices, LANES), F32)
    row = iota((32, width), 0)
    for step in range(mirrors // width):
        cols = pl.ds(step * width, width)
        owner, place = owner_of(mdest[:, cols], mslot[:, cols], n_bin, faces // n_bin)
        rank, seen = rank_chunk(owner, seen, tri)
        info_m[0:1, cols] = owner
        info_m[1:2, cols] = rank
        face = mface[:, cols]
        onehot = hot_rows(counted((LOW, width)), face & (LOW - 1))
        found = dot_plain(table, jnp.concatenate([onehot, onehot], 0))
        part = face >> 8
        nodes = jnp.zeros((32, width), F32)
        for h in range(high_count):
            nodes = jnp.where(part == h, found[32 * h : 32 * h + 32], nodes)
        first = 3 * mnode[:, cols]
        point = [
            jnp.sum(jnp.where(row == first + c, nodes, 0.0), 0, keepdims=True) for c in range(3)
        ]
        total = total + spread(owner, rank, point, place + 1.0, devices, LANES)
    send[:, 4 * ratio : 4 * ratio + 4, :] = total.reshape(devices, 4, LANES)


def lagrange(t):
    return (
        (t * (t - 1.0) * 0.5, 1.0 - t * t, t * (t + 1.0) * 0.5),
        (t - 0.5, -2.0 * t, t + 0.5),
    )


def surface(nodes, u, v):
    val_u, slope_u = lagrange(u)
    val_v, slope_v = lagrange(v)
    at, along_u, along_v = [], [], []
    for c in range(3):
        line = [sum(val_u[i] * nodes[3 * (i + 3 * j) + c] for i in range(3)) for j in range(3)]
        slope = [sum(slope_u[i] * nodes[3 * (i + 3 * j) + c] for i in range(3)) for j in range(3)]
        at.append(sum(val_v[j] * line[j] for j in range(3)))
        along_u.append(sum(val_v[j] * slope[j] for j in range(3)))
        along_v.append(sum(slope_v[j] * line[j] for j in range(3)))
    return val_u, val_v, at, along_u, along_v


def inner(a, b):
    return a[0] * b[0] + a[1] * b[1] + a[2] * b[2]


def contact(point, nodes, stiff):
    u = jnp.zeros_like(point[0])
    v = jnp.zeros_like(point[0])
    for _ in range(NEWTON):
        _, _, at, tu, tv = surface(nodes, u, v)
        off = [point[c] - at[c] for c in range(3)]
        a_uu, a_uv, a_vv = inner(tu, tu), inner(tu, tv), inner(tv, tv)
        b_u, b_v = inner(tu, off), inner(tv, off)
        inv = 1.0 / (a_uu * a_vv - a_uv * a_uv)
        u = jnp.clip(u + (a_vv * b_u - a_uv * b_v) * inv, -CLIP_EDGE, CLIP_EDGE)
        v = jnp.clip(v + (a_uu * b_v - a_uv * b_u) * inv, -CLIP_EDGE, CLIP_EDGE)
    val_u, val_v, at, tu, tv = surface(nodes, u, v)
    normal = [
        tu[1] * tv[2] - tu[2] * tv[1],
        tu[2] * tv[0] - tu[0] * tv[2],
        tu[0] * tv[1] - tu[1] * tv[0],
    ]
    scale = 1.0 / jnp.sqrt(inner(normal, normal))
    normal = [n * scale for n in normal]
    off = [point[c] - at[c] for c in range(3)]
    press = 0.5 * stiff * jnp.maximum(-inner(off, normal), 0.0)
    force = [press * n for n in normal]
    return force, val_u, val_v


def lookup(ref, row, low, high):
    result = None
    for h in range(ref.shape[1] // LANES):
        line = jnp.broadcast_to(ref[row : row + 1, h * LANES : (h + 1) * LANES], (8, LANES))
        value = [
            jnp.take_along_axis(line, part, axis=1, mode="promise_in_bounds") for part in low
        ]
        if h == 0:
            result = value
        else:
            result = [jnp.where(hi == h, v, r) for hi, v, r in zip(high, value, result)]
    return result


def contact_blocks(blocks, rows, order, coords, stiff, recv, ret, react, found, slot):
    def split(value):
        return [value[8 * n : 8 * n + 8] for n in range(len(blocks))]

    def far(first, c):
        return pl.ds(first + c, 8, stride=slot)

    def taken(c):
        return jnp.concatenate([recv[far(first, c), :] for first, dense in blocks], 0)

    def looked(ref, row, index):
        low = split(index & (LANES - 1))
        return jnp.concatenate(lookup(ref, row, low, split(index >> 7)), 0)

    point = [taken(c) for c in range(3)]
    code = taken(3)
    place = jnp.maximum(code - 1.0, 0.0).astype(jnp.int32)
    face = looked(order, 0, place)
    nodes = [looked(coords, r, face) for r in range(27)]
    strength = jnp.where(code > 0.5, looked(stiff, 0, face), 0.0)
    force, val_u, val_v = contact(point, nodes, strength)
    for n, (first, dense) in enumerate(blocks):
        part = slice(8 * n, 8 * n + 8)
        found[pl.ds(dense, 8), :] = face[part]
        for c in range(3):
            ret[far(first, c), :] = force[c][part]
        ret[far(first, 3), :] = jnp.zeros((8, LANES), F32)
    for j in range(3):
        for i in range(3):
            weight = -(val_u[i] * val_v[j])
            for c in range(3):
                row = 3 * (i + 3 * j) + c
                term = weight * force[c]
                for n, (first, dense) in enumerate(blocks):
                    react[pl.ds(row * rows + dense, 8), :] = term[8 * n : 8 * n + 8]


def scatter(rows, high_count, react, found, total):
    total[...] = jnp.zeros_like(total)

    def add(i, carry):
        lefts, rights = [], []
        numbers = counted((LOW, LANES))
        for q in range(8):
            p = i * 8 + q
            value = react[pl.ds(p, 32, stride=rows), :]
            upper, lower = pieces(value)
            both = jnp.concatenate([upper.astype(BF16), lower.astype(BF16)], 0)
            face = found[pl.ds(p, 1), :]
            high = jnp.broadcast_to((face >> 8).astype(F32), (16, LANES)).astype(BF16)
            high = jnp.concatenate([high] * 4, 0)
            parts = []
            for h in range(high_count):
                parts.append(jnp.where(high == float(h), both, jnp.zeros_like(both)))
            lefts.append(jnp.concatenate(parts, 0))
            rights.append(hot_rows(numbers, face & (LOW - 1)))
        total[...] += dot_lanes(jnp.concatenate(lefts, 1), jnp.concatenate(rights, 1))
        return carry

    lax.fori_loop(0, rows // 8, add, 0)


def fetch(key, lane, table, groups):
    width = key.shape[1]
    onehot = hot_rows(counted((LANES, width)), lane)
    spreaded = dot_plain(table, jnp.concatenate([onehot, onehot], 0))
    group = (iota((4 * groups, width), 0) >> 2).astype(F32)
    spreaded = jnp.where(group == key, spreaded, 0.0)
    result = jnp.sum(spreaded.reshape(groups // 2, 8, width), 0)
    return result + pltpu.roll(result, 4, 0)


def piece_table(value):
    return jnp.concatenate([p.astype(BF16) for p in pieces(value)], 1)


def collect(ratio, info_s, info_m, mface, mnode, back, slave_force, face_force, total, own):
    devices = back.shape[0]
    slaves = info_s.shape[1]
    mirrors = info_m.shape[1]
    high_count = face_force.shape[1] // LOW
    width = 256
    table = piece_table(back[:, 4 * ratio : 4 * ratio + 4, :].reshape(4 * devices, LANES))
    acc = None
    for step in range(mirrors // width):
        cols = pl.ds(step * width, width)
        result = fetch(info_m[0:1, cols], info_m[1:2, cols], table, devices)
        face = mface[:, cols]
        key = (face >> 8) * 16 + mnode[:, cols]
        rel = jnp.broadcast_to(key, (8, width)) - (iota((8, width), 0) >> 2)
        left = []
        for piece in pieces(result):
            for h in range(high_count):
                for j in range(5):
                    left.append(jnp.where(rel == 16 * h + 2 * j, piece, 0.0))
        left = jnp.concatenate(left, 0).astype(BF16)
        onehot = hot_rows(counted((LOW, width)), face & (LOW - 1))
        term = dot_lanes(left, onehot)
        acc = term if acc is None else acc + term
    own[...] = acc
    half = 40 * high_count
    for h in range(high_count):
        cols = slice(h * LOW, (h + 1) * LOW)
        mine = own[40 * h : 40 * h + 40, :] + own[half + 40 * h : half + 40 * h + 40, :]
        sent = total[64 * h : 64 * h + 27, :] + total[64 * h + 32 : 64 * h + 59, :]
        for n in range(9):
            face_force[3 * n : 3 * n + 3, cols] = (
                sent[3 * n : 3 * n + 3] + mine[4 * n : 4 * n + 3]
            )
    table = piece_table(back[:, 0 : 4 * ratio, :].reshape(4 * ratio * devices, LANES))
    for step in range(slaves // width):
        cols = pl.ds(step * width, width)
        result = fetch(info_s[0:1, cols], info_s[1:2, cols], table, devices * ratio)
        slave_force[:, cols] = result[0:3]


def step_kernel(n_mech, n_bin, ratio, *refs):
    inputs, (slave_force, face_force) = refs[:11], refs[11:13]
    local, rest = refs[13:24], refs[24:]
    (
        send, recv, ret, back, info_s, info_m, react, found, total, own,
        load_sem, go_send, go_recv, home_send, home_recv,
    ) = rest
    devices = n_mech * n_bin
    slot = send.shape[1]
    used = 4 * (ratio + 1)
    rows = (ratio + 1) * devices
    me = lax.axis_index("mech") * n_bin + lax.axis_index("bin")

    def device(i):
        return (i // n_bin, lax.rem(i, n_bin))

    barrier = pltpu.get_barrier_semaphore()

    def greet(i, carry):
        pl.semaphore_signal(
            barrier,
            inc=1,
            device_id=device(lax.rem(me + i, devices)),
            device_id_type=pl.DeviceIdType.MESH,
        )
        return carry

    loads = [
        pltpu.make_async_copy(inputs[n], local[n], load_sem.at[n]) for n in range(len(inputs))
    ]
    for load in loads:
        load.start()
    lax.fori_loop(1, devices, greet, 0)
    (count, pos, sdest, sslot, coords, mface, mnode, mdest, mslot, order, stiff) = local
    faces = coords.shape[1]
    for load in loads[:4]:
        load.wait()
    dispatch(n_bin, ratio, count, pos, sdest, sslot, send, info_s, faces)
    pl.semaphore_wait(barrier, devices - 1)
    halves = ((0, 4 * ratio), (4 * ratio, 4))

    def go(i, half):
        target = lax.rem(me + i, devices)
        start, size = halves[half]
        return pltpu.make_async_remote_copy(
            src_ref=send.at[target, pl.ds(start, size), :],
            dst_ref=recv.at[pl.ds(pl.multiple_of(i * slot, slot) + start, size), :],
            send_sem=go_send.at[half, i],
            recv_sem=go_recv.at[half, i],
            device_id=device(target),
            device_id_type=pl.DeviceIdType.MESH,
        )

    def home(i, half):
        target = lax.rem(me - i + devices, devices)
        start, size = halves[half]
        return pltpu.make_async_remote_copy(
            src_ref=ret.at[pl.ds(pl.multiple_of(i * slot, slot) + start, size), :],
            dst_ref=back.at[me, pl.ds(start, size), :],
            send_sem=home_send.at[half, i],
            recv_sem=home_recv.at[half, i],
            device_id=device(target),
            device_id_type=pl.DeviceIdType.MESH,
        )

    def start_go(half):
        def start(i, carry):
            go(i, half).start()
            return carry

        lax.fori_loop(1, devices, start, 0)

    start_go(0)
    for load in loads[4:]:
        load.wait()
    dispatch_mirrors(n_bin, ratio, coords, mface, mnode, mdest, mslot, send, info_m)
    start_go(1)
    recv[0:used, :] = send[me, 0:used, :]
    react[pl.ds(27 * rows, 5 * rows), :] = jnp.zeros((5 * rows, LANES), F32)
    tables = (rows, order, coords, stiff, recv, ret, react, found, slot)

    def peers(j, count, act):
        for q in range(count):
            i = j * count + q

            @pl.when(i > 0)
            def _():
                act(i)

    def group(j, carry):
        peers(j, 8, lambda i: go(i, 0).wait_recv())
        blocks = [
            (j * (8 * slot) + 4 * k, pl.multiple_of((j * ratio + k) * 8, 8)) for k in range(ratio)
        ]
        contact_blocks(blocks, *tables)
        peers(j, 8, lambda i: home(i, 0).start())
        return carry

    lax.fori_loop(0, devices // 8, group, 0)
    pair = 2 if devices % 16 == 0 else 1

    def mirror_group(j, carry):
        peers(j, 8 * pair, lambda i: go(i, 1).wait_recv())
        blocks = []
        for k in range(pair):
            g = j * pair + k
            dense = pl.multiple_of(ratio * devices + g * 8, 8)
            blocks.append((g * (8 * slot) + 4 * ratio, dense))
        contact_blocks(blocks, *tables)
        peers(j, 8 * pair, lambda i: home(i, 1).start())
        return carry

    lax.fori_loop(0, devices // (8 * pair), mirror_group, 0)
    back[me, 0:used, :] = ret[0:used, :]
    scatter(rows, faces // LOW, react, found, total)

    def finish(i, carry):
        for half in range(2):
            go(i, half).wait_send()
            home(i, half).wait_send()
            home(i, half).wait_recv()
        return carry

    lax.fori_loop(1, devices, finish, 0)
    collect(ratio, info_s, info_m, mface, mnode, back, slave_force, face_force, total, own)


def shards(
    face_coords,
    face_stiff,
    bin_order,
    slave_pos,
    slave_dest,
    face_slot,
    block_count,
    mirror_face,
    mirror_node,
    mirror_dest,
    mirror_slot,
):
    n_mech = lax.axis_size("mech")
    n_bin = lax.axis_size("bin")
    devices = n_mech * n_bin
    slaves = slave_pos.shape[1]
    mirrors = mirror_face.shape[0]
    faces = face_coords.shape[1]
    cap = 2 * slaves // devices
    ratio = -(-cap // LANES)
    rows = (ratio + 1) * devices
    slot = 8 * (-(-(ratio + 1) // 2))
    high_count = faces // LOW
    operands = (
        block_count,
        slave_pos,
        slave_dest.reshape(1, slaves),
        face_slot.reshape(1, slaves),
        face_coords,
        mirror_face.reshape(1, mirrors),
        mirror_node.reshape(1, mirrors),
        mirror_dest.reshape(1, mirrors),
        mirror_slot.reshape(1, mirrors),
        bin_order,
        face_stiff.reshape(1, faces),
    )
    vmem = pl.BlockSpec(memory_space=pltpu.VMEM)
    return pl.pallas_call(
        functools.partial(step_kernel, n_mech, n_bin, ratio),
        out_shape=(
            jax.ShapeDtypeStruct((3, slaves), F32),
            jax.ShapeDtypeStruct((27, faces), F32),
        ),
        in_specs=[pl.BlockSpec(memory_space=pltpu.HBM)] * len(operands),
        out_specs=(vmem, vmem),
        scratch_shapes=[pltpu.VMEM(o.shape, o.dtype) for o in operands]
        + [
            pltpu.VMEM((devices, slot, LANES), F32),
            pltpu.VMEM((devices * slot, LANES), F32),
            pltpu.VMEM((devices * slot, LANES), F32),
            pltpu.VMEM((devices, slot, LANES), F32),
            pltpu.VMEM((2, slaves), F32),
            pltpu.VMEM((2, mirrors), F32),
            pltpu.VMEM((32 * rows, LANES), F32),
            pltpu.VMEM((rows, LANES), jnp.int32),
            pltpu.VMEM((64 * high_count, LOW), F32),
            pltpu.VMEM((80 * high_count, LOW), F32),
            pltpu.SemaphoreType.DMA((len(operands),)),
        ]
        + [pltpu.SemaphoreType.DMA((2, devices))] * 4,
        compiler_params=pltpu.CompilerParams(
            vmem_limit_bytes=63 * 2**20, collective_id=0, has_side_effects=True
        ),
        name="contact_step",
    )(*operands)


def solution(mesh):
    both = ("mech", "bin")
    return jax.shard_map(
        shards,
        mesh=mesh,
        in_specs=(
            P(None, both),
            P(both),
            P(both, None),
            P(None, both),
            P(both, None),
            P(both),
            P(both, None),
            P(both),
            P(both),
            P(both, None),
            P(both),
        ),
        out_specs=(P(None, both), P(None, both)),
        check_vma=False,
    )
```
